32 devices in a mesh: fsdp: 32 (over z, y, x, core).
Axes of the slice: x: 2, y: 2, z: 4, core: 2. Of those that a mesh axis runs over, the one named last changes fastest.
Arguments:
- tokens: bfloat16 [65536, 768], P('fsdp'), may hold values from -6 to 6
- cotangent: bfloat16 [65536, 768], P('fsdp'), may hold values from -6 to 6
- segments: int32 [65536], P('fsdp'), may hold values from 0 to 1, as said below
- positions: int32 [65536], P('fsdp'), may hold values from 0 to 1999, as said below
- qkv_weight: float32 [768, 2304], P('fsdp'), may hold values from -0.21875 to 0.21875
- qkv_first: float32 [768, 2304], P('fsdp'), may hold values from -160 to 160
- qkv_second: float32 [768, 2304], P('fsdp'), may hold values from 1310 to 5461
- out_weight: float32 [768, 768], P('fsdp'), may hold values from -0.625 to 0.625
- out_first: float32 [768, 768], P('fsdp'), may hold values from -160 to 160
- out_second: float32 [768, 768], P('fsdp'), may hold values from 1310 to 5461
- in_weight: float32 [768, 2304], P('fsdp'), may hold values from -0.21875 to 0.21875
- in_first: float32 [768, 2304], P('fsdp'), may hold values from -160 to 160
- in_second: float32 [768, 2304], P('fsdp'), may hold values from 1310 to 5461
- down_weight: float32 [1152, 768], P('fsdp'), may hold values from -0.375 to 0.375
- down_first: float32 [1152, 768], P('fsdp'), may hold values from -160 to 160
- down_second: float32 [1152, 768], P('fsdp'), may hold values from 1310 to 5461
- norm_gains: float32 [2, 768], P(None, 'fsdp'), may hold values from 0.5 to 1.5
- gains_first: float32 [2, 768], P(None, 'fsdp'), may hold values from -160 to 160
- gains_second: float32 [2, 768], P(None, 'fsdp'), may hold values from 1310 to 5461
Outputs:
- activations: bfloat16 [65536, 768], P('fsdp')
- input_grad: float32 [65536, 768], P('fsdp')
- qkv_grad: float32 [768, 2304], P('fsdp')
- qkv_new: float32 [768, 2304], P('fsdp')
- qkv_first_new: float32 [768, 2304], P('fsdp')
- qkv_second_new: float32 [768, 2304], P('fsdp')
- out_grad: float32 [768, 768], P('fsdp')
- out_new: float32 [768, 768], P('fsdp')
- out_first_new: float32 [768, 768], P('fsdp')
- out_second_new: float32 [768, 768], P('fsdp')
- in_grad: float32 [768, 2304], P('fsdp')
- in_new: float32 [768, 2304], P('fsdp')
- in_first_new: float32 [768, 2304], P('fsdp')
- in_second_new: float32 [768, 2304], P('fsdp')
- down_grad: float32 [1152, 768], P('fsdp')
- down_new: float32 [1152, 768], P('fsdp')
- down_first_new: float32 [1152, 768], P('fsdp')
- down_second_new: float32 [1152, 768], P('fsdp')
- gains_grad: float32 [2, 768], P(None, 'fsdp')
- gains_delta: float32 [2, 768], P(None, 'fsdp')
- gains_first_new: float32 [2, 768], P(None, 'fsdp')
- gains_second_new: float32 [2, 768], P(None, 'fsdp')
The draws below stay inside these ranges and needn't reach their ends.
Inputs may be any that keep to these rules, and one draw needn't show every extreme that they name: `segments`: documents lie end to end over all 65536 tokens; the segment number is 0 on the first document and changes between 0 and 1 from each document to the next. Each document is 200 to 2000 tokens long, the last cut at the end, and both lengths occur. A document may run across packed sequences. `positions`: place of each token in its document counted from 0; it grows by one from token to token inside a document and starts again at 0 where the segment number changes.
All inputs are finite; a program needn't handle non-finite values.
Results may differ from the reference program's by a relative error of at most 0.019.
Values may be sent and summed in bfloat16 or wider, within the bound.
A program may use at most 256 MiB of HBM per device.

```python
import math
import jax
import jax.numpy as jnp
from jax import lax

D = 768
HEADS = 12
HEAD = 64
FF = 1152
SEQ = 512
BLK = 128
DOC_MIN = 200
DOC_MAX = 2000
STEP = 10
TOKENS = 65536


def document_stream(key):
    total_docs = TOKENS // DOC_MIN + 2
    doc_lengths = jax.random.randint(jax.random.fold_in(key, 11), (total_docs,), DOC_MIN, DOC_MAX + 1)
    doc_lengths = doc_lengths.at[0].set(DOC_MAX).at[1].set(DOC_MIN)
    doc_ends = jnp.cumsum(doc_lengths)
    places = jnp.arange(TOKENS)
    number = jnp.searchsorted(doc_ends, places, side='right').astype(jnp.int32)
    starts = doc_ends - doc_lengths
    return ((number % 2).astype(jnp.int32), (places - starts[number]).astype(jnp.int32))


def draw_segments(key, part):
    return document_stream(key)[0]


def draw_positions(key, part):
    return document_stream(key)[1]


def steps_of(own_key, shape, split, least, top_value):
    level, own = 1.0, jax.random.fold_in(own_key, 6)
    for position, blocks in split:
        heights = jnp.exp(jax.random.uniform(jax.random.fold_in(own, position), (blocks,), jnp.float32, least / len(split), top_value / len(split)))
        level = level * jnp.repeat(heights, shape[position] // blocks).reshape([-1 if axis == position else 1 for axis in range(len(shape))])
    return level


def normal_values(own_key, shape, scale, limit, split=(), dtype=jnp.bfloat16):
    gain = steps_of(own_key, shape, split, -0.22, 0.18) if split else 1.0
    values = jax.random.normal(own_key, shape, jnp.float32) * scale * gain
    return jnp.minimum(jnp.maximum(values, -limit), limit).astype(dtype)


def setup_inputs(seed: int = 0) -> dict:
    streams_of = jax.random.split(jax.random.key(seed), 20)
    return {
        "tokens": normal_values(streams_of[0], (TOKENS, D), 1.0, 6.0, ((0, 32),)),
        "cotangent": normal_values(streams_of[1], (TOKENS, D), 1.0, 6.0, ((0, 32),)),
        "segments": draw_segments(jax.random.fold_in(streams_of[19], 71), 0),
        "positions": draw_positions(jax.random.fold_in(streams_of[19], 71), 0),
        "qkv_weight": normal_values(streams_of[4], (D, 3 * D), D ** -0.5, 0.21875, ((0, 32),), jnp.float32),
        "qkv_first": normal_values(streams_of[5], (D, 3 * D), ((TOKENS // 81) ** 0.5), 160.0, ((0, 32),), jnp.float32),
        "qkv_second": jnp.clip(jnp.exp(math.log(5461.0) - 1.4276048 * jax.random.uniform(streams_of[6], (D, 3 * D), jnp.float32) ** steps_of(streams_of[6], (D, 3 * D), ((0, 32),), -0.2, 0.2)), 1310.0, 5461.0),
        "out_weight": normal_values(streams_of[7], (D, D), (D // 8) ** -0.5, 0.625, ((0, 32),), jnp.float32),
        "out_first": normal_values(streams_of[8], (D, D), ((TOKENS // 81) ** 0.5), 160.0, ((0, 32),), jnp.float32),
        "out_second": jnp.clip(jnp.exp(math.log(5461.0) - 1.4276048 * jax.random.uniform(streams_of[9], (D, D), jnp.float32) ** steps_of(streams_of[9], (D, D), ((0, 32),), -0.2, 0.2)), 1310.0, 5461.0),
        "in_weight": normal_values(streams_of[10], (D, 2 * FF), D ** -0.5, 0.21875, ((0, 32),), jnp.float32),
        "in_first": normal_values(streams_of[11], (D, 2 * FF), ((TOKENS // 81) ** 0.5), 160.0, ((0, 32),), jnp.float32),
        "in_second": jnp.clip(jnp.exp(math.log(5461.0) - 1.4276048 * jax.random.uniform(streams_of[12], (D, 2 * FF), jnp.float32) ** steps_of(streams_of[12], (D, 2 * FF), ((0, 32),), -0.2, 0.2)), 1310.0, 5461.0),
        "down_weight": normal_values(streams_of[13], (FF, D), (FF // 4) ** -0.5, 0.375, ((0, 32),), jnp.float32),
        "down_first": normal_values(streams_of[14], (FF, D), ((TOKENS // 81) ** 0.5), 160.0, ((0, 32),), jnp.float32),
        "down_second": jnp.clip(jnp.exp(math.log(5461.0) - 1.4276048 * jax.random.uniform(streams_of[15], (FF, D), jnp.float32) ** steps_of(streams_of[15], (FF, D), ((0, 32),), -0.2, 0.2)), 1310.0, 5461.0),
        "norm_gains": jnp.clip(1.0 + 0.1 * jax.random.normal(streams_of[16], (2, D), jnp.float32), 0.5, 1.5),
        "gains_first": normal_values(streams_of[17], (2, D), ((TOKENS // 81) ** 0.5), 160.0, ((1, 32),), jnp.float32),
        "gains_second": jnp.clip(jnp.exp(math.log(5461.0) - 1.4276048 * jax.random.uniform(streams_of[18], (2, D), jnp.float32) ** steps_of(streams_of[18], (2, D), ((1, 32),), -0.2, 0.2)), 1310.0, 5461.0),
    }


@jax.custom_vjp
def low(v):
    return lax.optimization_barrier(v.astype(jnp.bfloat16)).astype(jnp.float32)

@jax.custom_vjp
def low_back(v):
    return v

def low_keep(v):
    return (low(v), None)

def low_pass(kept, grad):
    return (grad,)

def back_keep(v):
    return (v, None)

def back_low(kept, grad):
    return (low(grad),)
low.defvjp(low_keep, low_pass)
low_back.defvjp(back_keep, back_low)
NORM_EPS = 1e-05
BETA_ONE = 0.9
BETA_TWO = 0.98
ADAM_EPS = 1e-06
LEARN_RATE = 0.1
WEIGHT_DECAY = 0.01
ROPE_BASE = 10000.0
MASKED = -1e+30

def product(left, right):
    return jnp.dot(left, right, precision=lax.Precision.HIGHEST, preferred_element_type=jnp.float32)

def layer_norm(values, norm_gain):
    center = values - lax.optimization_barrier(jnp.mean(values, axis=-1, keepdims=True))
    spread = lax.optimization_barrier(jnp.mean(center * center, axis=-1, keepdims=True))
    return center * lax.rsqrt(spread + NORM_EPS) * norm_gain

def rotate(values, cosine, sine):
    half_dim = values.shape[-1] // 2
    turned = jnp.concatenate([-values[..., half_dim:], values[..., :half_dim]], axis=-1)
    return values * cosine + turned * sine

def rope_tables(places):
    half_dim = HEAD // 2
    frequency = ROPE_BASE ** (-(jnp.arange(half_dim).astype(jnp.float32) * 2.0 / HEAD))
    angles = places.astype(jnp.float32)[:, None] * frequency[None, :]
    angles = jnp.concatenate([angles, angles], axis=-1)
    return (jnp.cos(angles)[:, None, :], jnp.sin(angles)[:, None, :])

def forward(hidden_in, param_vals, seq_segs, seq_places):
    qkv_low, out_low, in_low, down_low, gains_low = param_vals
    length = hidden_in.shape[0]
    normed = low(layer_norm(hidden_in, gains_low[0]))
    qkv_mixed = low_back(product(normed, qkv_low))
    cosine, sine = rope_tables(seq_places)
    query_heads = low(rotate(qkv_mixed[:, :D].reshape(length, HEADS, HEAD), cosine, sine))
    key_heads = low(rotate(qkv_mixed[:, D:2 * D].reshape(length, HEADS, HEAD), cosine, sine))
    value_heads = low(qkv_mixed[:, 2 * D:].reshape(length, HEADS, HEAD))
    scores = jnp.einsum('qhe,khe->hqk', query_heads, key_heads, precision=lax.Precision.HIGHEST) * HEAD ** (-0.5)
    scores = low_back(scores)
    places = jnp.arange(length)
    allowed = (seq_segs[:, None] == seq_segs[None, :]) & (jnp.abs(places[:, None] - places[None, :]) <= BLK // 2)
    scores = jnp.where(allowed[None], scores, MASKED)
    row_top = lax.optimization_barrier(jnp.max(scores, axis=-1, keepdims=True))
    exp_scores = jnp.exp(scores - row_top)
    prob_low = low(exp_scores / lax.optimization_barrier(jnp.sum(exp_scores, axis=-1, keepdims=True)))
    attended = jnp.einsum('hqk,khe->qhe', prob_low, value_heads, precision=lax.Precision.HIGHEST).reshape(length, D)
    attended = low_back(low(attended))
    residual = hidden_in + low_back(product(attended, out_low))
    normed_two = low(layer_norm(residual, gains_low[1]))
    gate_up = low_back(product(normed_two, in_low))
    active = low(jax.nn.gelu(gate_up[:, :FF], approximate=False) * gate_up[:, FF:])
    return residual + low_back(product(active, down_low))

def adam_step(master, weight_grad, moment_one, moment_two):
    first_new = BETA_ONE * moment_one + (1.0 - BETA_ONE) * weight_grad
    second_new = BETA_TWO * moment_two + (1.0 - BETA_TWO) * weight_grad * weight_grad
    first_hat = first_new / (1.0 - BETA_ONE ** STEP)
    second_hat = second_new / (1.0 - BETA_TWO ** STEP)
    master_new = master - LEARN_RATE * (first_hat / (jnp.sqrt(second_hat) + ADAM_EPS) + WEIGHT_DECAY * master)
    return (weight_grad, master_new, first_new, second_new)

def reference(tokens, cotangent, segments, positions, qkv_weight, qkv_first, qkv_second, out_weight, out_first, out_second, in_weight, in_first, in_second, down_weight, down_first, down_second, norm_gains, gains_first, gains_second):
    masters = (qkv_weight, out_weight, in_weight, down_weight, norm_gains)
    rounded = tuple((low(master) for master in masters))
    seq_total = TOKENS // SEQ
    hidden_all = tokens.astype(jnp.float32).reshape(seq_total, SEQ, D)
    cot_all = cotangent.astype(jnp.float32).reshape(seq_total, SEQ, D)
    seg_all = segments.reshape(seq_total, SEQ)
    place_all = positions.reshape(seq_total, SEQ)

    def one_sequence(running, seq_items):
        hidden_in, cot_seq, seq_segs, seq_places = seq_items

        def local_layer(hidden_val, param_vals):
            return forward(hidden_val, param_vals, seq_segs, seq_places)
        output, pullback = jax.vjp(local_layer, hidden_in, rounded)
        input_part, param_grads = pullback(cot_seq)
        running = jax.tree.map(jnp.add, running, param_grads)
        return (running, (output.astype(jnp.bfloat16), input_part))
    zero_grads = jax.tree.map(jnp.zeros_like, rounded)
    weight_grads, (outputs, input_grads) = lax.scan(one_sequence, zero_grads, (hidden_all, cot_all, seg_all, place_all))
    states = ((qkv_first, qkv_second), (out_first, out_second), (in_first, in_second), (down_first, down_second), (gains_first, gains_second))
    updated = [adam_step(master, weight_grad, pair_state[0], pair_state[1]) for master, weight_grad, pair_state in zip(masters, weight_grads, states)]
    gains_delta = updated[4][1] - norm_gains
    return (outputs.reshape(TOKENS, D), input_grads.reshape(TOKENS, D), updated[0][0], updated[0][1], updated[0][2], updated[0][3], updated[1][0], updated[1][1], updated[1][2], updated[1][3], updated[2][0], updated[2][1], updated[2][2], updated[2][3], updated[3][0], updated[3][1], updated[3][2], updated[3][3], updated[4][0], gains_delta, updated[4][2], updated[4][3])
```

```python
import jax
import jax.numpy as jnp
from jax import lax
from jax.experimental import pallas as pl
from jax.experimental.pallas import tpu as pltpu
from jax.sharding import PartitionSpec as P

D = 768
HEADS = 12
HEAD = 64
FF = 1152
SEQ = 512
BLK = 128
STEP = 10

NORM_EPS = 1e-05
BETA_ONE = 0.9
BETA_TWO = 0.98
ADAM_EPS = 1e-06
LEARN_RATE = 0.1
WEIGHT_DECAY = 0.01
ROPE_BASE = 10000.0
MASKED = -1e30

GROUP = 4
WIDE = GROUP * HEAD
GROUPS = HEADS // GROUP
BLOCKS = SEQ // BLK
SPAN = 2 * BLK
KEY_AT = tuple(min(max(b * BLK - BLK // 2, 0), SEQ - SPAN) for b in range(BLOCKS))
FF_CHUNKS = ((0, 256), (256, 256), (512, 256), (768, 256), (1024, 128))
VMEM = 60 * 1024 * 1024
BF = jnp.bfloat16
F32 = jnp.float32


def mm(a, b):
    return lax.dot_general(a, b, (((1,), (0,)), ((), ())), preferred_element_type=F32)


def mm_nt(a, b):
    return lax.dot_general(a, b, (((1,), (1,)), ((), ())), preferred_element_type=F32)


def mm_tn(a, b):
    return lax.dot_general(a, b, (((0,), (0,)), ((), ())), preferred_element_type=F32)


def norm_parts(x):
    center = x - jnp.mean(x, axis=-1, keepdims=True)
    scale = lax.rsqrt(jnp.mean(center * center, axis=-1, keepdims=True) + NORM_EPS)
    return center * scale, scale


def norm_back(e, gain, xh, scale):
    f = e * gain
    return (
        f - jnp.mean(f, axis=-1, keepdims=True) - xh * jnp.mean(f * xh, axis=-1, keepdims=True)
    ) * scale


def turned(u):
    half = HEAD // 2
    lane = lax.broadcasted_iota(jnp.int32, u.shape, 1)
    return jnp.where(
        lane % HEAD < half, pltpu.roll(u, u.shape[1] - half, 1), pltpu.roll(u, half, 1)
    )


def twice(t):
    return jnp.concatenate([t, t], axis=1)


def head_masks(dtype):
    lane = lax.broadcasted_iota(jnp.int32, (1, WIDE), 1)
    return [jnp.where(lane // HEAD == j, 1.0, 0.0).astype(dtype) for j in range(GROUP)]


def spread_heads(block, masks):
    return jnp.concatenate([block * m for m in masks], axis=0)


def gather_heads(stacked, masks):
    total = stacked[:BLK] * masks[0]
    for j in range(1, GROUP):
        total = total + stacked[j * BLK : (j + 1) * BLK] * masks[j]
    return total


def fill_bias(segc_ref, segr_ref, bias_ref):
    for b in range(BLOCKS):
        ks = KEY_AT[b]
        key_at = ks + lax.broadcasted_iota(jnp.int32, (SPAN, BLK), 0)
        query_at = b * BLK + lax.broadcasted_iota(jnp.int32, (SPAN, BLK), 1)
        near = jnp.abs(key_at - query_at) <= BLK // 2
        same = segc_ref[ks : ks + SPAN, :] == segr_ref[0, :, b * BLK : (b + 1) * BLK]
        bias_ref[b] = jnp.where(near & same, 0.0, MASKED)


def bias_of(bias_ref, b):
    one = bias_ref[b]
    return jnp.concatenate([one] * GROUP, axis=1)


def attend_kernel(
    tok_ref, gain_ref, wqkv_ref, wo_ref, cos_ref, sin_ref, segc_ref, segr_ref,
    q_ref, k_ref, v_ref, att_ref, lse_ref, res_ref, bias_ref, normed_ref,
):
    xh, _ = norm_parts(tok_ref[...].astype(F32))
    normed_ref[...] = (xh * gain_ref[...]).astype(BF)
    fill_bias(segc_ref, segr_ref, bias_ref)
    masks_low, masks = head_masks(BF), head_masks(F32)

    def group(g, carry):
        at = pl.multiple_of(g * WIDE, WIDE)
        cosine, sine = twice(cos_ref[...]), twice(sin_ref[...])
        normed = normed_ref[...]
        u = mm(normed, wqkv_ref[:, pl.ds(at, WIDE)])
        q_ref[:, pl.ds(at, WIDE)] = (
            (u * cosine + turned(u) * sine) * HEAD ** (-0.5)
        ).astype(BF)
        u = mm(normed, wqkv_ref[:, pl.ds(D + at, WIDE)])
        k_ref[:, pl.ds(at, WIDE)] = (u * cosine + turned(u) * sine).astype(BF)
        v_ref[:, pl.ds(at, WIDE)] = mm(normed, wqkv_ref[:, pl.ds(2 * D + at, WIDE)]).astype(BF)
        for b in range(BLOCKS):
            ks, qs = KEY_AT[b], b * BLK
            heads_q = spread_heads(q_ref[qs : qs + BLK, pl.ds(at, WIDE)], masks_low)
            keys = k_ref[ks : ks + SPAN, pl.ds(at, WIDE)]
            vals = v_ref[ks : ks + SPAN, pl.ds(at, WIDE)]
            scores = mm_nt(keys, heads_q) + bias_of(bias_ref, b)
            top = jnp.max(scores, axis=0, keepdims=True)
            grown = jnp.exp(scores - top)
            total = jnp.sum(grown, axis=0, keepdims=True)
            prob = (grown * (1.0 / total)).astype(BF)
            att_ref[qs : qs + BLK, pl.ds(at, WIDE)] = gather_heads(
                mm_tn(prob, vals), masks
            ).astype(BF)
            lse_ref[g * BLOCKS + b] = top + jnp.log(total)
        return carry

    lax.fori_loop(0, GROUPS, group, 0)
    res_ref[...] = tok_ref[...].astype(F32) + mm(att_ref[...], wo_ref[...])


def feed_kernel(
    res_ref, cot_ref, gain_ref, wi_ref, wd_ref,
    act_ref, dres_ref, gin_ref, gdown_ref, ggain_ref,
    n2_ref, n2t_ref, out_ref, gn_ref, gin_acc, gdown_acc,
):
    step = pl.program_id(0)

    @pl.when(step == 0)
    def _():
        gin_acc[...] = jnp.zeros_like(gin_acc)
        gdown_acc[...] = jnp.zeros_like(gdown_acc)
        ggain_ref[...] = jnp.zeros_like(ggain_ref)

    xh, _ = norm_parts(res_ref[...])
    n2 = xh * gain_ref[...]
    n2_ref[...] = n2.astype(BF)
    n2t_ref[...] = n2.T.astype(BF)
    for i, (at, width) in enumerate(FF_CHUNKS):
        wi_gate = wi_ref[:, at : at + width]
        wi_up = wi_ref[:, FF + at : FF + at + width]
        wd = wd_ref[at : at + width, :]
        cot = cot_ref[...]
        gate = mm(n2_ref[...], wi_gate)
        up = mm(n2_ref[...], wi_up)
        phi = 0.5 + 0.5 * lax.erf(gate * (0.5**0.5))
        gelu = gate * phi
        active = gelu * up
        active_low = active.astype(BF)
        slope = phi + gate * jnp.exp(-0.5 * gate * gate) * 0.3989422804014327
        ga = mm_nt(cot, wd)
        dgate = (ga * up * slope).astype(BF)
        dup = (ga * gelu).astype(BF)
        out = mm(active_low, wd)
        gn = mm_nt(dgate, wi_gate) + mm_nt(dup, wi_up)
        if i == 0:
            out_ref[...] = out
            gn_ref[...] = gn
        else:
            out_ref[...] += out
            gn_ref[...] += gn
        gdown_acc[at : at + width, :] += mm_tn(active_low, cot)
        gin_acc[:, at : at + width] += mm(n2t_ref[...], dgate)
        gin_acc[:, FF + at : FF + at + width] += mm(n2t_ref[...], dup)
    res = res_ref[...]
    act_ref[...] = (res + out_ref[...]).astype(BF)
    xh, scale = norm_parts(res)
    gn = gn_ref[...]
    dres_ref[...] = cot_ref[...].astype(F32) + norm_back(gn, gain_ref[...], xh, scale)
    ggain_ref[...] += jnp.sum(gn * xh, axis=0, keepdims=True)

    @pl.when(step == pl.num_programs(0) - 1)
    def _():
        gin_ref[...] = gin_acc[...].astype(BF)
        gdown_ref[...] = gdown_acc[...].astype(BF)


def attend_back_kernel(
    dres_ref, tok_ref, gain_ref, wo_ref, cos_ref, sin_ref, segc_ref, segr_ref,
    q_ref, k_ref, v_ref, att_ref, lse_ref,
    gm_ref, gqkv_ref, gout_ref,
    bias_ref, normt_ref, ga_ref, dq_ref, dk_ref, dv_ref, gqkv_acc, gout_acc,
):
    step = pl.program_id(0)

    @pl.when(step == 0)
    def _():
        gqkv_acc[...] = jnp.zeros_like(gqkv_acc)
        gout_acc[...] = jnp.zeros_like(gout_acc)

    dres_low = dres_ref[...].astype(BF)
    ga_ref[...] = mm_nt(dres_low, wo_ref[...]).astype(BF)
    gout_acc[...] += mm_tn(att_ref[...], dres_low)
    xh, _ = norm_parts(tok_ref[...].astype(F32))
    normt_ref[...] = (xh * gain_ref[...]).T.astype(BF)
    fill_bias(segc_ref, segr_ref, bias_ref)
    masks_low, masks = head_masks(BF), head_masks(F32)

    def group(g, carry):
        at = pl.multiple_of(g * WIDE, WIDE)
        dk_ref[...] = jnp.zeros_like(dk_ref)
        dv_ref[...] = jnp.zeros_like(dv_ref)
        for b in range(BLOCKS):
            ks, qs = KEY_AT[b], b * BLK
            heads_q = spread_heads(q_ref[qs : qs + BLK, pl.ds(at, WIDE)], masks_low)
            heads_g = spread_heads(ga_ref[qs : qs + BLK, pl.ds(at, WIDE)], masks_low)
            keys = k_ref[ks : ks + SPAN, pl.ds(at, WIDE)]
            vals = v_ref[ks : ks + SPAN, pl.ds(at, WIDE)]
            scores = mm_nt(keys, heads_q) + bias_of(bias_ref, b)
            prob = jnp.exp(scores - lse_ref[g * BLOCKS + b])
            dv_ref[ks : ks + SPAN, :] += mm(prob.astype(BF), heads_g)
            dprob = mm_nt(vals, heads_g)
            inner = jnp.sum(prob * dprob, axis=0, keepdims=True)
            dscore = (prob * (dprob - inner)).astype(BF)
            dk_ref[ks : ks + SPAN, :] += mm(dscore, heads_q)
            dq_ref[qs : qs + BLK, :] = gather_heads(mm_tn(dscore, keys), masks)
        cosine, sine = twice(cos_ref[...]), twice(sin_ref[...])
        u = dq_ref[...] * HEAD ** (-0.5)
        part = (u * cosine - turned(u) * sine).astype(BF)
        gm_ref[:, pl.ds(at, WIDE)] = part
        gqkv_acc[:, pl.ds(at, WIDE)] += mm(normt_ref[...], part)
        u = dk_ref[...]
        part = (u * cosine - turned(u) * sine).astype(BF)
        gm_ref[:, pl.ds(D + at, WIDE)] = part
        gqkv_acc[:, pl.ds(D + at, WIDE)] += mm(normt_ref[...], part)
        part = dv_ref[...].astype(BF)
        gm_ref[:, pl.ds(2 * D + at, WIDE)] = part
        gqkv_acc[:, pl.ds(2 * D + at, WIDE)] += mm(normt_ref[...], part)
        return carry

    lax.fori_loop(0, GROUPS, group, 0)

    @pl.when(step == pl.num_programs(0) - 1)
    def _():
        gqkv_ref[...] = gqkv_acc[...].astype(BF)
        gout_ref[...] = gout_acc[...].astype(BF)


def input_kernel(gm_ref, tok_ref, dres_ref, gain_ref, wqkv_ref, gin_ref, ggain_ref):
    @pl.when(pl.program_id(0) == 0)
    def _():
        ggain_ref[...] = jnp.zeros_like(ggain_ref)

    xh, scale = norm_parts(tok_ref[...].astype(F32))
    e = mm_nt(gm_ref[...], wqkv_ref[...])
    gin_ref[...] = dres_ref[...] + norm_back(e, gain_ref[...], xh, scale)
    ggain_ref[...] += jnp.sum(e * xh, axis=0, keepdims=True)


def rows_of(width, height=SEQ):
    return pl.BlockSpec((height, width), lambda i: (i, 0))


def whole(*shape):
    return pl.BlockSpec(shape, lambda i: (0,) * len(shape), pipeline_mode=pl.Buffered(1))


def kept(*shape):
    return pl.BlockSpec(shape, lambda i: (0,) * len(shape))


def shape_of(shape, dtype):
    return jax.ShapeDtypeStruct(shape, dtype)


def run(kernel, steps, in_specs, out_specs, out_shape, scratch, flops, moved):
    return pl.pallas_call(
        kernel,
        grid=(steps,),
        in_specs=in_specs,
        out_specs=out_specs,
        out_shape=out_shape,
        scratch_shapes=scratch,
        cost_estimate=pl.CostEstimate(flops=flops, bytes_accessed=moved, transcendentals=0),
        compiler_params=pltpu.CompilerParams(
            dimension_semantics=("arbitrary",), vmem_limit_bytes=VMEM
        ),
    )


def rope_tables(places):
    half_dim = HEAD // 2
    frequency = ROPE_BASE ** (-(jnp.arange(half_dim).astype(F32) * 2.0 / HEAD))
    angles = places.astype(F32)[:, None] * frequency[None, :]
    cosine, sine = jnp.cos(angles), jnp.sin(angles)
    return (
        jnp.concatenate([cosine] * 4, axis=1),
        jnp.concatenate([-sine, sine, -sine, sine], axis=1),
    )


def adam_step(master, weight_grad, moment_one, moment_two):
    first_new = BETA_ONE * moment_one + (1.0 - BETA_ONE) * weight_grad
    second_new = BETA_TWO * moment_two + (1.0 - BETA_TWO) * weight_grad * weight_grad
    first_hat = first_new / (1.0 - BETA_ONE**STEP)
    second_hat = second_new / (1.0 - BETA_TWO**STEP)
    master_new = master - LEARN_RATE * (
        first_hat / (jnp.sqrt(second_hat) + ADAM_EPS) + WEIGHT_DECAY * master
    )
    return (weight_grad, master_new, first_new, second_new)


def shards(
    tokens,
    cotangent,
    segments,
    positions,
    qkv_weight,
    qkv_first,
    qkv_second,
    out_weight,
    out_first,
    out_second,
    in_weight,
    in_first,
    in_second,
    down_weight,
    down_first,
    down_second,
    norm_gains,
    gains_first,
    gains_second,
):
    devices = lax.axis_size("fsdp")
    rows = tokens.shape[0]
    seqs = rows // SEQ
    own_out, own_gain, own_down = out_weight.shape[0], norm_gains.shape[1], down_weight.shape[0]
    pack = own_out + 8
    down_pack = (own_down + 7) // 8 * 8

    qkv_low = lax.all_gather(qkv_weight.astype(BF), "fsdp", axis=0, tiled=True)
    gain_rows = jnp.pad(norm_gains, ((0, 6), (0, D - own_gain)))
    packed = jnp.concatenate([out_weight, gain_rows], axis=0).astype(BF)
    packed = lax.all_gather(packed, "fsdp", axis=0, tiled=True).reshape(devices, pack, D)
    out_low = packed[:, :own_out].reshape(D, D)
    gains = packed[:, own_out : own_out + 2, :own_gain].astype(F32)
    gains = gains.transpose(1, 0, 2).reshape(2, D)
    in_low = lax.all_gather(in_weight.astype(BF), "fsdp", axis=0, tiled=True)
    down_rows = jnp.pad(down_weight, ((0, down_pack - own_down), (0, 0))).astype(BF)
    down_low = lax.all_gather(down_rows, "fsdp", axis=0, tiled=True)
    down_low = down_low.reshape(devices, down_pack, D)[:, :own_down].reshape(FF, D)

    gain_one, gain_two = gains[0:1], gains[1:2]
    cosine, sine = rope_tables(positions)
    seg_col = segments.reshape(rows, 1)
    seg_row = segments.reshape(seqs, 1, SEQ)
    seg_row_spec = pl.BlockSpec((1, 1, SEQ), lambda i: (i, 0, 0))
    lse_spec = pl.BlockSpec((None, GROUPS * BLOCKS, 1, GROUP * BLK), lambda i: (i, 0, 0, 0))
    bias_scratch = pltpu.VMEM((BLOCKS, SPAN, BLK), F32)
    low_rows = shape_of((rows, D), BF)

    q, k, v, attended, lse, residual = run(
        attend_kernel,
        seqs,
        [rows_of(D), whole(1, D), whole(D, 3 * D), whole(D, D), rows_of(BLK), rows_of(BLK),
         rows_of(1), seg_row_spec],
        [rows_of(D)] * 4 + [lse_spec, rows_of(D)],
        [low_rows] * 4
        + [shape_of((seqs, GROUPS * BLOCKS, 1, GROUP * BLK), F32), shape_of((rows, D), F32)],
        [bias_scratch, pltpu.VMEM((SEQ, D), BF)],
        2 * rows * D * (4 * D) + 4 * rows * HEADS * SPAN * WIDE,
        rows * D * 14,
    )(tokens, gain_one, qkv_low, out_low, cosine, sine, seg_col, seg_row)

    activations, dres, gin, gdown, ggain_two = run(
        feed_kernel,
        seqs,
        [rows_of(D), rows_of(D), whole(1, D), whole(D, 2 * FF), whole(FF, D)],
        [rows_of(D), rows_of(D), kept(D, 2 * FF), kept(FF, D), kept(1, D)],
        [low_rows, shape_of((rows, D), F32), shape_of((D, 2 * FF), BF), shape_of((FF, D), BF),
         shape_of((1, D), F32)],
        [pltpu.VMEM((SEQ, D), BF), pltpu.VMEM((D, SEQ), BF), pltpu.VMEM((SEQ, D), F32),
         pltpu.VMEM((SEQ, D), F32), pltpu.VMEM((D, 2 * FF), F32), pltpu.VMEM((FF, D), F32)],
        2 * rows * D * FF * 9,
        rows * D * 12,
    )(residual, cotangent, gain_two, in_low, down_low)

    owned_in = lax.psum_scatter(gin, "fsdp", scatter_dimension=0, tiled=True)
    gdown = jnp.pad(
        gdown.reshape(devices, own_down, D), ((0, 0), (0, down_pack - own_down), (0, 0))
    ).reshape(devices * down_pack, D)
    owned_down = lax.psum_scatter(gdown, "fsdp", scatter_dimension=0, tiled=True)[:own_down]

    gmixed, gqkv, gout = run(
        attend_back_kernel,
        seqs,
        [rows_of(D), rows_of(D), whole(1, D), whole(D, D), rows_of(BLK), rows_of(BLK),
         rows_of(1), seg_row_spec, rows_of(D), rows_of(D), rows_of(D), rows_of(D), lse_spec],
        [rows_of(3 * D), kept(D, 3 * D), kept(D, D)],
        [shape_of((rows, 3 * D), BF), shape_of((D, 3 * D), BF), shape_of((D, D), BF)],
        [bias_scratch, pltpu.VMEM((D, SEQ), BF), pltpu.VMEM((SEQ, D), BF),
         pltpu.VMEM((SEQ, WIDE), F32), pltpu.VMEM((SEQ, WIDE), F32), pltpu.VMEM((SEQ, WIDE), F32),
         pltpu.VMEM((D, 3 * D), F32), pltpu.VMEM((D, D), F32)],
        2 * rows * D * (5 * D) + 10 * rows * HEADS * SPAN * WIDE,
        rows * D * 22,
    )(dres, tokens, gain_one, out_low, cosine, sine, seg_col, seg_row, q, k, v, attended, lse)

    owned_qkv = lax.psum_scatter(gqkv, "fsdp", scatter_dimension=0, tiled=True)

    input_grad, ggain_one = run(
        input_kernel,
        seqs,
        [rows_of(3 * D), rows_of(D), rows_of(D), whole(1, D), whole(D, 3 * D)],
        [rows_of(D), kept(1, D)],
        [shape_of((rows, D), F32), shape_of((1, D), F32)],
        [],
        2 * rows * D * 3 * D,
        rows * D * 16,
    )(gmixed, tokens, dres, gain_one, qkv_low)

    ggain = jnp.concatenate([ggain_one, ggain_two], axis=0)
    ggain = ggain.reshape(2, devices, own_gain).transpose(1, 0, 2).astype(BF)
    ggain = jnp.pad(ggain, ((0, 0), (0, 6), (0, D - own_gain)))
    packed = jnp.concatenate([gout.reshape(devices, own_out, D), ggain], axis=1)
    packed = packed.reshape(devices * pack, D)
    owned_pack = lax.psum_scatter(packed, "fsdp", scatter_dimension=0, tiled=True)
    owned_out = owned_pack[:own_out].astype(F32)
    owned_gain = owned_pack[own_out : own_out + 2, :own_gain].astype(F32)

    qkv_state = adam_step(qkv_weight, owned_qkv.astype(F32), qkv_first, qkv_second)
    out_state = adam_step(out_weight, owned_out, out_first, out_second)
    in_state = adam_step(in_weight, owned_in.astype(F32), in_first, in_second)
    down_state = adam_step(down_weight, owned_down.astype(F32), down_first, down_second)
    gains_state = adam_step(norm_gains, owned_gain, gains_first, gains_second)
    gains_delta = gains_state[1] - norm_gains
    return (
        activations,
        input_grad,
        *qkv_state,
        *out_state,
        *in_state,
        *down_state,
        gains_state[0],
        gains_delta,
        gains_state[2],
        gains_state[3],
    )


def solution(mesh):
    return jax.shard_map(
        shards,
        mesh=mesh,
        in_specs=(
            P("fsdp", None),
            P("fsdp", None),
            P("fsdp"),
            P("fsdp"),
            P("fsdp", None),
            P("fsdp", None),
            P("fsdp", None),
            P("fsdp", None),
            P("fsdp", None),
            P("fsdp", None),
            P("fsdp", None),
            P("fsdp", None),
            P("fsdp", None),
            P("fsdp", None),
            P("fsdp", None),
            P("fsdp", None),
            P(None, "fsdp"),
            P(None, "fsdp"),
            P(None, "fsdp"),
        ),
        out_specs=(
            P("fsdp", None),
            P("fsdp", None),
            P("fsdp", None),
            P("fsdp", None),
            P("fsdp", None),
            P("fsdp", None),
            P("fsdp", None),
            P("fsdp", None),
            P("fsdp", None),
            P("fsdp", None),
            P("fsdp", None),
            P("fsdp", None),
            P("fsdp", None),
            P("fsdp", None),
            P("fsdp", None),
            P("fsdp", None),
            P("fsdp", None),
            P("fsdp", None),
            P(None, "fsdp"),
            P(None, "fsdp"),
            P(None, "fsdp"),
            P(None, "fsdp"),
        ),
        check_vma=False,
    )
```
